256 devices in a mesh: blk: 64 (over z, y_hi, x), col: 4 (over y_lo, core).
Axes of the slice: x: 4, y: 4 (y_hi: 2, y_lo: 2; y = y_hi * 2 + y_lo), z: 8, core: 2. Of those that a mesh axis runs over, the one named last changes fastest.
Arguments:
- points: float32 [16, 65536], P(None, 'blk'), may hold values from -5 to 5
- lengths: float32 [16], replicated, may hold values from 2 to 4
- noise: float32 [65536], P('blk'), may hold values from 0.5 to 2
- outscale: float32 [1], replicated, may hold values from 0.02 to 0.1
- solution: float32 [32, 65536], P('col', 'blk'), may hold values from -6 to 6
- residual: float32 [32, 65536], P('col', 'blk'), may hold values from -26 to 26
- direction: float32 [32, 65536], P('col', 'blk'), may hold values from -31 to 31
Outputs:
- solution_next: float32 [32, 65536], P('col', 'blk')
- residual_next: float32 [32, 65536], P('col', 'blk')
- direction_next: float32 [32, 65536], P('col', 'blk')
The draws below stay inside these ranges and needn't reach their ends.
All inputs are finite; a program needn't handle non-finite values.
Results may differ from the reference program's by a relative error of at most 0.0003.
Values may be sent and summed in bfloat16 or wider, within the bound.
No kernel may reach another device: no remote copies, remote signals or barrier semaphores. Data moves between devices by JAX's collectives and lax.ppermute only.
A program may use at most 64 MiB of HBM per device.

```python
import math
import jax
import jax.numpy as jnp
from jax import lax

DIM = 16
COLS = 32
POINTS = 65536


def field_scale():
    rows = jnp.arange(COLS, dtype=jnp.float32)[:, None]
    spots = jnp.arange(POINTS, dtype=jnp.float32)[None, :]
    return 0.2 * 10.0 ** (spots / (POINTS - 1)) * 10.0 ** (0.5 * rows / (COLS - 1))


def draw_residual(key, part):
    key = jax.random.fold_in(key, 11)
    values = jax.random.truncated_normal(key, -4.0, 4.0, (COLS, POINTS), jnp.float32)
    return values * field_scale()


def draw_direction(key, part):
    key = jax.random.fold_in(key, 23)
    signs = jax.random.randint(jax.random.fold_in(key, 7), (COLS, 1), 0, 2).astype(jnp.float32) * 2.0 - 1.0
    values = jax.random.truncated_normal(key, -4.0, 4.0, (COLS, POINTS), jnp.float32)
    values = values + 0.8 * signs
    return values * field_scale()


def steps_of(own_key, extent, split, low, top_value):
    gain, own = 1.0, jax.random.fold_in(own_key, 6)
    for dim, blocks in split:
        heights = jnp.exp(jax.random.uniform(jax.random.fold_in(own, dim), (blocks,), jnp.float32, low / len(split), top_value / len(split)))
        gain = gain * jnp.repeat(heights, extent[dim] // blocks).reshape([-1 if axis == dim else 1 for axis in range(len(extent))])
    return gain


def gaussian(rng, shape, spread, limit, shards=(), kind=jnp.bfloat16):
    values = jax.random.normal(rng, shape, jnp.float32) * spread
    if len(shards) > 0:
        values = steps_of(rng, shape, shards, -0.22, 0.18) * values
    return jnp.clip(values, min=-limit, max=limit).astype(kind)


def setup_inputs(seed: int = 0) -> dict:
    splits = jax.random.split(jax.random.key(seed), 8)
    points = gaussian(splits[0], (DIM, POINTS), 1.0, 5.0, ((1, 64),), jnp.float32)
    lengths = jnp.clip(jnp.exp(jax.random.uniform(splits[1], (DIM,), jnp.float32, math.log(2.0), math.log(4.0))), 2.0, 4.0)
    noise = jnp.clip(jnp.exp(math.log(2.0) - 1.3862944 * jax.random.uniform(splits[2], (POINTS,), jnp.float32) ** steps_of(splits[2], (POINTS,), ((0, 64),), -0.2, 0.2)), 0.5, 2.0)
    outscale = jnp.clip(jnp.exp(jax.random.uniform(splits[3], (1,), jnp.float32, math.log(0.02), math.log(0.1))), 0.02, 0.1)
    solution = gaussian(splits[4], (COLS, POINTS), 1.0, 6.0, ((0, 4), (1, 64)), jnp.float32)
    residual = draw_residual(jax.random.fold_in(splits[7], 71), 0)
    direction = draw_direction(jax.random.fold_in(splits[7], 71), 0)
    return {"points": points, "lengths": lengths, "noise": noise, "outscale": outscale, "solution": solution, "residual": residual, "direction": direction}


def matern_tile(left, right, amplitude):
    cross = lax.dot_general(left, right, (((0,), (0,)), ((), ())), precision=lax.Precision.HIGHEST, preferred_element_type=jnp.float32)
    left_sq = lax.optimization_barrier(jnp.sum(left * left, axis=0))
    right_sq = lax.optimization_barrier(jnp.sum(right * right, axis=0))
    dist_sq = jnp.maximum(left_sq[:, None] + right_sq[None, :] - 2.0 * cross, 0.0)
    radius = jnp.sqrt(5.0 * dist_sq)
    return (amplitude * (1.0 + radius + radius * radius / 3.0) * jnp.exp(-radius)).astype(jnp.bfloat16)

def reference(points, lengths, noise, outscale, solution, residual, direction):
    scaled = points / lengths[:, None]
    lowered = direction.astype(jnp.bfloat16)
    block_rows = math.gcd(POINTS, 512)
    count = POINTS // block_rows
    pieces = scaled.reshape(DIM, count, block_rows).transpose(1, 0, 2)

    def one_block(piece):
        kernel_tile = matern_tile(scaled, piece, outscale[0])
        return jnp.dot(lowered, kernel_tile, preferred_element_type=jnp.float32)
    products = lax.map(one_block, pieces)
    image = products.transpose(1, 0, 2).reshape(COLS, POINTS) + noise[None, :] * direction
    norm_now = lax.optimization_barrier(jnp.sum(residual * residual, axis=1))
    curve = lax.optimization_barrier(jnp.sum(direction * image, axis=1))
    alpha = norm_now / curve
    solution_next = solution + alpha[:, None] * direction
    residual_next = residual - alpha[:, None] * image
    norm_next = lax.optimization_barrier(jnp.sum(residual_next * residual_next, axis=1))
    direction_next = residual_next + (norm_next / norm_now)[:, None] * direction
    return (solution_next, residual_next, direction_next)
```

```python
import functools
import math

import jax
import jax.numpy as jnp
from jax import lax
from jax.experimental import pallas as pl
from jax.experimental.pallas import tpu as pltpu
from jax.sharding import Mesh, PartitionSpec as P

F32 = jnp.float32
BF16 = jnp.bfloat16
KAPPA = 1.0 / math.log(2.0)
SHIFT = -1.5 * KAPPA
CONST = 0.75 * KAPPA * KAPPA
FACTOR = math.exp(1.5) / (3.0 * KAPPA * KAPPA)
TINY = 1e-30

BLK = ("z", "yh", "x")
COL = ("yl", "core")
NEAR = ("x", "yl", "core")
FAR = ("z", "yh")


def split3(value):
    high = value.astype(BF16).astype(F32)
    rest = value - high
    middle = rest.astype(BF16).astype(F32)
    return high, middle, rest - middle


def matern(dist):
    dist = jnp.maximum(dist, TINY)
    t = SHIFT - dist * lax.rsqrt(dist)
    return ((t * t + CONST) * jnp.exp2(t)).astype(BF16)


def stack_rows(rows, width):
    index = lax.broadcasted_iota(jnp.int32, (16, width), 0)
    total = jnp.zeros((16, width), F32)
    for place, row in enumerate(rows):
        total = jnp.where(index == place, row, total)
    return total


def image_kernel(tile_i, tile_j, rows_ref, cols_ref, out_ref, row_f, col_f, low, dist_s, kern_s):
    groups, _, width = rows_ref.shape
    pieces, _, piece = cols_ref.shape
    count_i = groups * width
    count_j = pieces * piece

    def row_features(g, _):
        value = rows_ref[g]
        norm = split3(jnp.sum(value * value, axis=0, keepdims=True))
        one = jnp.ones((1, width), F32)
        misc = stack_rows((*norm, one, one, one), width)
        parts = jnp.concatenate([*split3(value), misc], axis=0)
        row_f[:, pl.ds(pl.multiple_of(g * width, width), width)] = parts.astype(BF16)
        return 0

    lax.fori_loop(0, groups, row_features, 0)

    def col_features(p, _):
        value = cols_ref[p, 32:48, :].astype(F32)
        norm = split3(jnp.sum(value * value, axis=0, keepdims=True))
        one = jnp.ones((1, piece), F32)
        misc = stack_rows((one, one, one, *norm), piece)
        cross = -2.0 * value
        parts = jnp.concatenate([cross, cross, cross, misc], axis=0)
        place = pl.ds(pl.multiple_of(p * piece, piece), piece)
        col_f[place, :] = parts.T.astype(BF16)
        low[:, place] = cols_ref[p, 0:32, :]
        return 0

    lax.fori_loop(0, pieces, col_features, 0)

    per = count_j // tile_j
    steps = (count_i // tile_i) * per
    per_group = width // tile_i

    def spot_i(step):
        return pl.ds(pl.multiple_of((step // per) * tile_i, tile_i), tile_i)

    def spot_j(step):
        return pl.ds(pl.multiple_of((step % per) * tile_j, tile_j), tile_j)

    def distances(step, slot):
        dist_s[slot] = jnp.dot(
            col_f[spot_j(step), :], row_f[:, spot_i(step)], preferred_element_type=F32
        )

    def accumulate(step, slot):
        tile = step // per
        group = tile // per_group
        place = pl.ds(pl.multiple_of((tile % per_group) * tile_i, tile_i), tile_i)
        out_ref[group, :, place] += jnp.dot(
            low[:, spot_j(step)], kern_s[slot], preferred_element_type=F32
        )

    out_ref[...] = jnp.zeros_like(out_ref)
    kern_s[1] = jnp.zeros((tile_j, tile_i), BF16)
    distances(0, 0)

    def one(step, slot):
        accumulate(jnp.maximum(step - 1, 0), 1 - slot)
        distances(jnp.minimum(step + 1, steps - 1), 1 - slot)
        for a in range(0, tile_j, 16):
            kern_s[slot, a : a + 16, :] = matern(dist_s[slot, a : a + 16, :])

    def two(pair, _):
        one(2 * pair, 0)
        one(2 * pair + 1, 1)
        return 0

    lax.fori_loop(0, steps // 2, two, 0)
    accumulate(steps - 1, 1)


def kernel_image(rows, cols, tile_i=256, tile_j=512):
    groups, _, width = rows.shape
    pieces, _, piece = cols.shape
    count_i, count_j = groups * width, pieces * piece
    vmem = pl.BlockSpec(memory_space=pltpu.VMEM)
    return pl.pallas_call(
        functools.partial(image_kernel, tile_i, tile_j),
        out_shape=jax.ShapeDtypeStruct((groups, 32, width), F32),
        in_specs=[vmem, vmem],
        out_specs=vmem,
        scratch_shapes=[
            pltpu.VMEM((64, count_i), BF16),
            pltpu.VMEM((count_j, 64), BF16),
            pltpu.VMEM((32, count_j), BF16),
            pltpu.VMEM((2, tile_j, tile_i), F32),
            pltpu.VMEM((2, tile_j, tile_i), BF16),
        ],
        compiler_params=pltpu.CompilerParams(vmem_limit_bytes=40 * 2**20),
        cost_estimate=pl.CostEstimate(
            flops=2 * count_i * count_j * 96,
            bytes_accessed=4 * 1024 * 1024,
            transcendentals=2 * count_i * count_j,
        ),
        name="kernel_image",
    )(rows, cols)


def spread(value, axes, count):
    return lax.all_to_all(
        jnp.broadcast_to(value[None], (count, *value.shape)), axes, 0, 0, tiled=True
    )


def local(points, lengths, noise, outscale, solution, residual, direction):
    far = lax.axis_size(FAR)
    near = lax.axis_size(NEAR)
    cols = lax.axis_size(COL)
    own, count = direction.shape
    piece = count // cols

    scaled = points * ((KAPPA * math.sqrt(5.0)) / lengths)[:, None]
    lowered = direction.astype(BF16)
    columns = lax.all_to_all(lowered, COL, 1, 0, tiled=True)
    some = lax.dynamic_slice_in_dim(scaled, lax.axis_index(COL) * piece, piece, 1)
    packet = jnp.concatenate([columns, some.astype(BF16)], axis=0)
    packets = spread(packet, FAR, far)
    rows = spread(scaled, "x", lax.axis_size("x"))

    partial = kernel_image(rows, packets)
    partial = lax.all_to_all(partial.reshape(near, own, count), NEAR, 0, 0, tiled=True)
    image = (FACTOR * outscale[0]) * jnp.sum(partial, axis=0) + noise[None, :] * direction

    sums = jnp.concatenate(
        [
            jnp.sum(residual * residual, axis=1),
            jnp.sum(direction * image, axis=1),
            jnp.sum(residual * image, axis=1),
            jnp.sum(image * image, axis=1),
        ]
    )
    sums = jnp.sum(spread(sums, BLK, lax.axis_size(BLK)), axis=0).reshape(4, own)
    norm_now, curve, mixed, square = sums[0], sums[1], sums[2], sums[3]
    alpha = norm_now / curve
    norm_next = jnp.maximum(norm_now - alpha * (2.0 * mixed - alpha * square), 0.0)
    solution_next = solution + alpha[:, None] * direction
    residual_next = residual - alpha[:, None] * image
    direction_next = residual_next + (norm_next / norm_now)[:, None] * direction
    return (solution_next, residual_next, direction_next)


def solution(mesh):
    fine = Mesh(mesh.devices.reshape(8, 2, 4, 2, 2), (*BLK, *COL))
    in_specs = (
        P(None, BLK),
        P(),
        P(BLK),
        P(),
        P(COL, BLK),
        P(COL, BLK),
        P(COL, BLK),
    )
    out_specs = (P(COL, BLK), P(COL, BLK), P(COL, BLK))
    return jax.shard_map(local, mesh=fine, in_specs=in_specs, out_specs=out_specs, check_vma=False)
```

```python
import functools
import math

import jax
import jax.numpy as jnp
from jax import lax
from jax.experimental import pallas as pl
from jax.experimental.pallas import tpu as pltpu
from jax.sharding import Mesh, PartitionSpec as P

F32 = jnp.float32
BF16 = jnp.bfloat16
KAPPA = 1.0 / math.log(2.0)
SHIFT = -1.5 * KAPPA
CONST = 0.75 * KAPPA * KAPPA
FACTOR = math.exp(1.5) / (3.0 * KAPPA * KAPPA)
TINY = 1e-30

BLK = ("z", "yh", "x")
COL = ("yl", "core")
NEAR = ("x", "yl", "core")
FAR = ("z", "yh")


def split3(value):
    high = value.astype(BF16).astype(F32)
    rest = value - high
    middle = rest.astype(BF16).astype(F32)
    return high, middle, rest - middle


def stack_rows(rows, width):
    index = lax.broadcasted_iota(jnp.int32, (16, width), 0)
    total = jnp.zeros((16, width), F32)
    for place, row in enumerate(rows):
        total = jnp.where(index == place, row, total)
    return total


def row_kernel(x_ref, own_ref, *refs):
    others, out_ref = refs[:-1], refs[-1]
    width = own_ref.shape[1]
    groups = len(others) + 1
    for step, ref in enumerate((own_ref, *others)):
        value = ref[...]
        norm = split3(jnp.sum(value * value, axis=0, keepdims=True))
        one = jnp.ones((1, width), F32)
        misc = stack_rows((*norm, one, one, one), width)
        parts = jnp.concatenate([*split3(value), misc], axis=0)
        group = lax.rem(x_ref[0] + step, groups)
        out_ref[:, pl.ds(pl.multiple_of(group * width, width), width)] = parts.astype(BF16)


def row_features(index, blocks):
    count = sum(block.shape[1] for block in blocks)
    vmem = pl.BlockSpec(memory_space=pltpu.VMEM)
    return pl.pallas_call(
        row_kernel,
        out_shape=jax.ShapeDtypeStruct((64, count), BF16),
        in_specs=[pl.BlockSpec(memory_space=pltpu.SMEM)] + [vmem] * len(blocks),
        out_specs=vmem,
        name="row_features",
    )(index, *blocks)


def image_kernel(tile_i, tile_j, core_ref, rows_ref, packets_ref, keep_ref, send_ref, *scratch):
    col_f, low, dist_s, expo_s, kern_s = scratch
    pieces = packets_ref.shape[0] // 4
    piece = 256
    half = piece // 2
    count_i = rows_ref.shape[1]
    count_j = pieces * piece
    width = keep_ref.shape[2]
    core = core_ref[0]

    def col_features(p, _):
        parts = [packets_ref[4 * p + q].astype(F32) for q in range(4)]
        value = jnp.concatenate(
            [
                jnp.concatenate([parts[0][:, piece:], parts[1][:, piece:]], axis=1),
                jnp.concatenate([parts[2][:, piece:], parts[3][:, piece:]], axis=1),
            ],
            axis=0,
        )
        norm = split3(jnp.sum(value * value, axis=0, keepdims=True))
        one = jnp.ones((1, piece), F32)
        misc = stack_rows((one, one, one, *norm), piece)
        cross = -2.0 * value
        place = pl.ds(pl.multiple_of(p * piece, piece), piece)
        col_f[place, :] = jnp.concatenate([cross, cross, cross, misc], axis=0).T.astype(BF16)
        mine = [packets_ref[4 * p + core].astype(F32), packets_ref[4 * p + 2 + core].astype(F32)]
        rest = [packets_ref[4 * p + 1 - core].astype(F32), packets_ref[4 * p + 3 - core].astype(F32)]
        columns = jnp.concatenate([part[:, :piece] for part in mine + rest], axis=0)
        low[:, place] = columns.astype(BF16)
        return 0

    lax.fori_loop(0, pieces, col_features, 0)

    per = count_j // tile_j
    steps = (count_i // tile_i) * per
    per_group = width // tile_i

    def spot_i(step):
        return pl.ds(pl.multiple_of((step // per) * tile_i, tile_i), tile_i)

    def spot_j(step):
        return pl.ds(pl.multiple_of((step % per) * tile_j, tile_j), tile_j)

    def distances(step, slot):
        dist_s[slot] = jnp.dot(
            col_f[spot_j(step), :], rows_ref[:, spot_i(step)], preferred_element_type=F32
        )

    def exponents(slot, a):
        dist = jnp.maximum(dist_s[slot, a : a + 16, :], TINY)
        expo_s[slot, a : a + 16, :] = SHIFT - dist * lax.rsqrt(dist)

    def entries(slot, a):
        t = expo_s[slot, a : a + 16, :]
        kern_s[slot, a : a + 16, :] = ((t * t + CONST) * jnp.exp2(t)).astype(BF16)

    def accumulate(step, slot):
        tile = step // per
        group = tile // per_group
        place = pl.ds(pl.multiple_of((tile % per_group) * tile_i, tile_i), tile_i)
        product = jnp.dot(low[:, spot_j(step)], kern_s[slot], preferred_element_type=F32)
        keep_ref[group, :, place] += product[:16]
        send_ref[group, :, place] += product[16:]

    keep_ref[...] = jnp.zeros_like(keep_ref)
    send_ref[...] = jnp.zeros_like(send_ref)
    kern_s[1] = jnp.zeros((tile_j, tile_i), BF16)
    distances(0, 0)
    distances(1, 1)
    for a in range(0, tile_j, 16):
        exponents(0, a)

    def one(step, slot):
        accumulate(jnp.maximum(step - 1, 0), 1 - slot)
        for a in range(0, tile_j, 16):
            entries(slot, a)
            exponents(1 - slot, a)
        distances(jnp.minimum(step + 2, steps - 1), slot)

    def four(index, _):
        for k in range(4):
            one(4 * index + k, k % 2)
        return 0

    lax.fori_loop(0, steps // 4, four, 0)
    accumulate(steps - 1, 1)


def kernel_image(core, rows, packets, width, tile_i=256, tile_j=1024):
    count_i, count_j = rows.shape[1], packets.shape[0] // 4 * 256
    vmem = pl.BlockSpec(memory_space=pltpu.VMEM)
    shape = jax.ShapeDtypeStruct((count_i // width, 16, width), F32)
    return pl.pallas_call(
        functools.partial(image_kernel, tile_i, tile_j),
        out_shape=(shape, shape),
        in_specs=[pl.BlockSpec(memory_space=pltpu.SMEM), vmem, vmem],
        out_specs=(vmem, vmem),
        scratch_shapes=[
            pltpu.VMEM((count_j, 64), BF16),
            pltpu.VMEM((32, count_j), BF16),
            pltpu.VMEM((2, tile_j, tile_i), F32),
            pltpu.VMEM((2, tile_j, tile_i), F32),
            pltpu.VMEM((2, tile_j, tile_i), BF16),
        ],
        compiler_params=pltpu.CompilerParams(vmem_limit_bytes=40 * 2**20),
        cost_estimate=pl.CostEstimate(
            flops=2 * count_i * count_j * 96,
            bytes_accessed=4 * 1024 * 1024,
            transcendentals=2 * count_i * count_j,
        ),
        name="kernel_image",
    )(core, rows, packets)


def spread(value, axes, count):
    return lax.all_to_all(
        jnp.broadcast_to(value[None], (count, *value.shape)), axes, 0, 0, tiled=True
    )


def local(points, lengths, noise, outscale, solution, residual, direction):
    far, near, line = lax.axis_size(FAR), lax.axis_size(NEAR), lax.axis_size("x")
    cols = lax.axis_size(COL)
    own, count = direction.shape
    piece = count // cols
    yl, core = lax.axis_index("yl"), lax.axis_index("core")

    scaled = points * ((KAPPA * math.sqrt(5.0)) / lengths)[:, None]
    blocks = [scaled] + [
        lax.ppermute(scaled, "x", [(i, (i - step) % line) for i in range(line)])
        for step in range(1, line)
    ]
    rows = row_features(lax.axis_index("x")[None], blocks)

    lowered = direction.astype(BF16).reshape(own, cols, piece)
    part = lax.dynamic_slice_in_dim(scaled, yl * 8, 8, 0).reshape(8, cols, piece)
    part = lax.dynamic_slice_in_dim(part, core * (piece // 2), piece // 2, 2).astype(BF16)
    packet = jnp.concatenate([lowered, part], axis=2).transpose(1, 0, 2)
    packets = jnp.broadcast_to(packet[None], (far, *packet.shape))
    packets = packets.reshape(far * cols, *packet.shape[1:])
    packets = lax.all_to_all(packets, FAR + COL, 0, 0, tiled=True)

    keep, send = kernel_image(core[None], rows, packets, count)
    keep = keep + lax.ppermute(send, "core", [(0, 1), (1, 0)])
    partial = keep.reshape(near // 2, own, count)
    partial = lax.all_to_all(partial, ("x", "yl"), 0, 0, tiled=True)
    image = (FACTOR * outscale[0]) * jnp.sum(partial, axis=0) + noise[None, :] * direction

    sums = jnp.concatenate(
        [
            jnp.sum(residual * residual, axis=1),
            jnp.sum(direction * image, axis=1),
            jnp.sum(residual * image, axis=1),
            jnp.sum(image * image, axis=1),
        ]
    )
    sums = spread(sums, BLK, lax.axis_size(BLK))
    sums = jnp.sum(sums, axis=0).reshape(4, own)
    norm_now, curve, mixed, square = sums[0], sums[1], sums[2], sums[3]
    alpha = norm_now / curve
    norm_next = jnp.maximum(norm_now - alpha * (2.0 * mixed - alpha * square), 0.0)
    solution_next = solution + alpha[:, None] * direction
    residual_next = residual - alpha[:, None] * image
    direction_next = residual_next + (norm_next / norm_now)[:, None] * direction
    return (solution_next, residual_next, direction_next)


def solution(mesh):
    fine = Mesh(mesh.devices.reshape(8, 2, 4, 2, 2), (*BLK, *COL))
    in_specs = (
        P(None, BLK),
        P(),
        P(BLK),
        P(),
        P(COL, BLK),
        P(COL, BLK),
        P(COL, BLK),
    )
    out_specs = (P(COL, BLK), P(COL, BLK), P(COL, BLK))
    return jax.shard_map(local, mesh=fine, in_specs=in_specs, out_specs=out_specs, check_vma=False)
```

```python
import functools
import math

import jax
import jax.numpy as jnp
from jax import lax
from jax.experimental import pallas as pl
from jax.experimental.pallas import tpu as pltpu
from jax.sharding import Mesh, PartitionSpec as P

F32 = jnp.float32
BF16 = jnp.bfloat16
KAPPA = 1.0 / math.log(2.0)
SHIFT = -1.5 * KAPPA
CONST = 0.75 * KAPPA * KAPPA
FACTOR = math.exp(1.5) / (3.0 * KAPPA * KAPPA)
TINY = 1e-30

BLK = ("z", "yh", "x")
COL = ("yl", "core")
FAR = ("z", "yh")


def split3(value):
    high = value.astype(BF16).astype(F32)
    rest = value - high
    middle = rest.astype(BF16).astype(F32)
    return high, middle, rest - middle


def stack_rows(rows, width):
    index = lax.broadcasted_iota(jnp.int32, (16, width), 0)
    total = jnp.zeros((16, width), F32)
    for place, row in enumerate(rows):
        total = jnp.where(index == place, row, total)
    return total


def row_kernel(*refs):
    count = len(refs) // 2
    for ref, out_ref in zip(refs[:count], refs[count:]):
        value = ref[...]
        norm = split3(jnp.sum(value * value, axis=0, keepdims=True))
        one = jnp.ones((1, value.shape[1]), F32)
        misc = stack_rows((*norm, one, one, one), value.shape[1])
        out_ref[...] = jnp.concatenate([*split3(value), misc], axis=0).astype(BF16)


def row_features(blocks):
    vmem = pl.BlockSpec(memory_space=pltpu.VMEM)
    return pl.pallas_call(
        row_kernel,
        out_shape=tuple(jax.ShapeDtypeStruct((64, block.shape[1]), BF16) for block in blocks),
        in_specs=[vmem] * len(blocks),
        out_specs=(vmem,) * len(blocks),
        compiler_params=pltpu.CompilerParams(vmem_limit_bytes=8 * 2**20),
        name="row_features",
    )(*blocks)


def col_kernel(place_ref, packets_ref, col_f, low):
    yl = place_ref[0]
    pieces = packets_ref.shape[0] // 2
    piece = packets_ref.shape[2] // 3

    def features(p):
        parts = [packets_ref[q * pieces + p].astype(F32) for q in range(2)]
        value = jnp.concatenate([part[:, 2 * piece :] for part in parts], axis=0)
        norm = split3(jnp.sum(value * value, axis=0, keepdims=True))
        one = jnp.ones((1, piece), F32)
        misc = stack_rows((one, one, one, *norm), piece)
        cross = -2.0 * value
        place = pl.ds(pl.multiple_of(p * piece, piece), piece)
        col_f[place, :] = jnp.concatenate([cross, cross, cross, misc], axis=0).T.astype(BF16)
        parts = [packets_ref[q * pieces + p].astype(F32) for q in (yl, 1 - yl)]
        columns = [part[:, k * piece : (k + 1) * piece] for k in range(2) for part in parts]
        low[:, place] = jnp.concatenate(columns, axis=0).astype(BF16)

    def some(index, _):
        for k in range(4):
            features(4 * index + k)
        return 0

    lax.fori_loop(0, pieces // 4, some, 0)


def col_features(place, packets):
    vmem = pl.BlockSpec(memory_space=pltpu.VMEM)
    count = packets.shape[0] * packets.shape[2] // 6
    return pl.pallas_call(
        col_kernel,
        out_shape=(jax.ShapeDtypeStruct((count, 64), BF16), jax.ShapeDtypeStruct((32, count), BF16)),
        in_specs=[pl.BlockSpec(memory_space=pltpu.SMEM), vmem],
        out_specs=(vmem, vmem),
        compiler_params=pltpu.CompilerParams(vmem_limit_bytes=8 * 2**20),
        name="col_features",
    )(place, packets)


def image_kernel(groups, tile_i, tile_j, *refs):
    rows_refs, (col_f, low), out_refs = refs[:groups], refs[groups : groups + 2], refs[groups + 2 : 2 * groups + 2]
    rows, total, dist_s, expo_s, kern_s = refs[2 * groups + 2 :]
    count_j = low.shape[1]
    width = out_refs[0].shape[1]
    count_i = groups * width
    for g in range(groups):
        rows[:, g * width : (g + 1) * width] = rows_refs[g][...]
    per = count_j // tile_j
    steps = (count_i // tile_i) * per
    per_group = width // tile_i

    def spot_i(step):
        return pl.ds(pl.multiple_of((step // per) * tile_i, tile_i), tile_i)

    def spot_j(step):
        return pl.ds(pl.multiple_of((step % per) * tile_j, tile_j), tile_j)

    def distances(step, slot):
        dist_s[slot] = jnp.dot(
            col_f[spot_j(step), :], rows[:, spot_i(step)], preferred_element_type=F32
        )

    def exponents(slot, a):
        dist = jnp.maximum(dist_s[slot, a : a + 16, :], TINY)
        expo_s[slot, a : a + 16, :] = SHIFT - dist * lax.rsqrt(dist)

    def entries(slot, a):
        t = expo_s[slot, a : a + 16, :]
        kern_s[slot, a : a + 16, :] = ((t * t + CONST) * jnp.exp2(t)).astype(BF16)

    def accumulate(step, slot):
        tile = step // per
        group = tile // per_group
        place = pl.ds(pl.multiple_of((tile % per_group) * tile_i, tile_i), tile_i)
        product = jnp.dot(low[:, spot_j(step)], kern_s[slot], preferred_element_type=F32)
        total[group, :, place] += product

    total[...] = jnp.zeros_like(total)
    kern_s[1] = jnp.zeros((tile_j, tile_i), BF16)
    distances(0, 0)
    distances(1, 1)
    for a in range(0, tile_j, 16):
        exponents(0, a)

    def one(step, slot):
        accumulate(jnp.maximum(step - 1, 0), 1 - slot)
        for a in range(0, tile_j, 16):
            entries(slot, a)
            exponents(1 - slot, a)
        distances(jnp.minimum(step + 2, steps - 1), slot)

    def four(index, _):
        for k in range(4):
            one(4 * index + k, k % 2)
        return 0

    lax.fori_loop(0, steps // 4, four, 0)
    accumulate(steps - 1, 1)
    for g in range(groups):
        out_refs[g][...] = total[g]


def kernel_image(rows, col_f, low, tile_i=256, tile_j=1024):
    groups, width, count_j = len(rows), rows[0].shape[1], low.shape[1]
    count_i = groups * width
    vmem = pl.BlockSpec(memory_space=pltpu.VMEM)
    return pl.pallas_call(
        functools.partial(image_kernel, groups, tile_i, tile_j),
        out_shape=(jax.ShapeDtypeStruct((32, width), F32),) * groups,
        in_specs=[vmem] * (groups + 2),
        out_specs=(vmem,) * groups,
        scratch_shapes=[
            pltpu.VMEM((64, count_i), BF16),
            pltpu.VMEM((groups, 32, width), F32),
            pltpu.VMEM((2, tile_j, tile_i), F32),
            pltpu.VMEM((2, tile_j, tile_i), F32),
            pltpu.VMEM((2, tile_j, tile_i), BF16),
        ],
        compiler_params=pltpu.CompilerParams(vmem_limit_bytes=24 * 2**20),
        cost_estimate=pl.CostEstimate(
            flops=2 * count_i * count_j * 96,
            bytes_accessed=4 * 1024 * 1024,
            transcendentals=2 * count_i * count_j,
        ),
        name="kernel_image",
    )(*rows, col_f, low)


def add_kernel(count, *refs):
    total = refs[0][...]
    for ref in refs[1:count]:
        total = total + ref[...]
    half = total.shape[0] // 2
    refs[count][...] = total[:half]
    refs[count + 1][...] = total[half:]


def add_parts(parts):
    vmem = pl.BlockSpec(memory_space=pltpu.VMEM)
    columns, width = parts[0].shape
    return pl.pallas_call(
        functools.partial(add_kernel, len(parts)),
        out_shape=(jax.ShapeDtypeStruct((columns // 2, width), F32),) * 2,
        in_specs=[vmem] * len(parts),
        out_specs=(vmem,) * 2,
        compiler_params=pltpu.CompilerParams(vmem_limit_bytes=8 * 2**20),
        name="add_parts",
    )(*parts)


def pack_kernel(far, place_ref, lengths_ref, points_ref, direction_ref, other_ref, scaled_ref, packets_ref):
    yl, core = place_ref[0], place_ref[1]
    dims, count = points_ref.shape
    piece = count // 4
    index = lax.broadcasted_iota(jnp.int32, (dims, 128), 0)
    lengths = jnp.ones((dims, 128), F32)
    for d in range(dims):
        lengths = jnp.where(index == d, lengths_ref[d], lengths)
    scale = ((KAPPA * math.sqrt(5.0)) / lengths)[:, :1]
    scaled_ref[...] = points_ref[...] * scale
    for q in range(2):
        here = pl.ds(pl.multiple_of((2 * q + core) * piece, piece), piece)
        half = scaled_ref[pl.ds(pl.multiple_of(yl * 8, 8), 8), here]
        packet = jnp.concatenate([direction_ref[:, here], other_ref[:, here], half], axis=1).astype(BF16)
        for n in range(far):
            packets_ref[q * far + n] = packet


def pack(far, place, lengths, points, direction, other):
    vmem = pl.BlockSpec(memory_space=pltpu.VMEM)
    smem = pl.BlockSpec(memory_space=pltpu.SMEM)
    own, count = direction.shape
    return pl.pallas_call(
        functools.partial(pack_kernel, far),
        out_shape=(
            jax.ShapeDtypeStruct(points.shape, F32),
            jax.ShapeDtypeStruct((2 * far, own, 3 * count // 4), BF16),
        ),
        in_specs=[smem, smem, vmem, vmem, vmem],
        out_specs=(vmem, vmem),
        compiler_params=pltpu.CompilerParams(vmem_limit_bytes=8 * 2**20),
        name="pack",
    )(place, lengths, points, direction, other)


def sums_kernel(scale_ref, noise_ref, direction_ref, residual_ref, solution_ref, *refs):
    parts, (image_ref, same_ref, out_ref) = refs[:-3], refs[-3:]
    direction, residual = direction_ref[...], residual_ref[...]
    total = parts[0][...]
    for part in parts[1:]:
        total = total + part[...]
    image = (FACTOR * scale_ref[0]) * total + noise_ref[...] * direction
    image_ref[...] = image
    same_ref[...] = solution_ref[...]
    own = direction.shape[0]
    lane = lax.broadcasted_iota(jnp.int32, (own, 128), 1)
    row = lax.broadcasted_iota(jnp.int32, (own, 128), 0)
    sums = jnp.zeros((own, 128), F32)
    for k, term in enumerate((residual * residual, direction * image, residual * image, image * image)):
        sums = jnp.where(lane == k * own + row, jnp.sum(term, axis=1, keepdims=True), sums)
    out_ref[...] = jnp.broadcast_to(jnp.sum(sums, axis=0, keepdims=True), out_ref.shape)


def column_sums(scale, parts, noise, direction, residual, solution, copies):
    vmem = pl.BlockSpec(memory_space=pltpu.VMEM)
    block = jax.ShapeDtypeStruct(direction.shape, F32)
    return pl.pallas_call(
        sums_kernel,
        out_shape=(block, block, jax.ShapeDtypeStruct((copies, 128), F32)),
        in_specs=[pl.BlockSpec(memory_space=pltpu.SMEM)] + [vmem] * (4 + len(parts)),
        out_specs=(vmem,) * 3,
        compiler_params=pltpu.CompilerParams(vmem_limit_bytes=8 * 2**20),
        name="column_sums",
    )(scale, noise, direction, residual, solution, *parts)


def local(points, lengths, noise, outscale, solution, residual, direction):
    far, line = lax.axis_size(FAR), lax.axis_size("x")
    own, count = direction.shape
    swap = [(0, 1), (1, 0)]

    place = jnp.stack([lax.axis_index("yl"), lax.axis_index("core")])
    other = lax.ppermute(direction, "core", swap)
    scaled, packets = pack(far, place, lengths, points, direction, other)
    packets = lax.all_to_all(packets, ("yl", *FAR), 0, 0, tiled=True)
    blocks = [scaled] + [
        lax.ppermute(scaled, "x", [(i, (i - step) % line) for i in range(line)])
        for step in range(1, line)
    ]
    rows = row_features(blocks)

    def send(value, step):
        return lax.ppermute(value, "x", [(i, (i + step) % line) for i in range(line)])

    columns = col_features(place, packets)
    image3, image2, image1 = kernel_image((rows[3], rows[2], rows[1]), *columns)
    image3, image2, image1 = send(image3, 3), send(image2, 2), send(image1, 1)
    (image0,) = kernel_image((rows[0],), *columns)
    keep, rest = add_parts((image0, image1, image2, image3))
    keep, rest = add_parts((keep, lax.ppermute(rest, "core", swap)))
    parts = [keep, lax.ppermute(rest, "yl", swap)]
    image, solution, sums = column_sums(
        outscale, parts, noise[None, :], direction, residual, solution, lax.axis_size(BLK)
    )
    sums = lax.all_to_all(sums, BLK, 0, 0, tiled=True)
    sums = jnp.sum(sums, axis=0)[: 4 * own].reshape(4, own)
    norm_now, curve, mixed, square = sums[0], sums[1], sums[2], sums[3]
    alpha = norm_now / curve
    norm_next = jnp.maximum(norm_now - alpha * (2.0 * mixed - alpha * square), 0.0)
    solution_next = solution + alpha[:, None] * direction
    residual_next = residual - alpha[:, None] * image
    direction_next = residual_next + (norm_next / norm_now)[:, None] * direction
    return (solution_next, residual_next, direction_next)


def solution(mesh):
    fine = Mesh(mesh.devices.reshape(8, 2, 4, 2, 2), (*BLK, *COL))
    in_specs = (
        P(None, BLK),
        P(),
        P(BLK),
        P(),
        P(COL, BLK),
        P(COL, BLK),
        P(COL, BLK),
    )
    out_specs = (P(COL, BLK), P(COL, BLK), P(COL, BLK))
    return jax.shard_map(local, mesh=fine, in_specs=in_specs, out_specs=out_specs, check_vma=False)
```

```python
import functools
import math

import jax
import jax.numpy as jnp
from jax import lax
from jax.experimental import pallas as pl
from jax.experimental.pallas import tpu as pltpu
from jax.sharding import Mesh, PartitionSpec as P

F32 = jnp.float32
BF16 = jnp.bfloat16
KAPPA = 1.0 / math.log(2.0)
SHIFT = -1.5 * KAPPA
CONST = 0.75 * KAPPA * KAPPA
FACTOR = math.exp(1.5) / (3.0 * KAPPA * KAPPA)
TINY = 1e-30

BLK = ("z", "yh", "x")
COL = ("yl", "core")
FAR = ("z",)


def split3(value):
    high = value.astype(BF16).astype(F32)
    rest = value - high
    middle = rest.astype(BF16).astype(F32)
    return high, middle, rest - middle


def stack_rows(rows, width):
    index = lax.broadcasted_iota(jnp.int32, (16, width), 0)
    total = jnp.zeros((16, width), F32)
    for place, row in enumerate(rows):
        total = jnp.where(index == place, row, total)
    return total


def row_kernel(*refs):
    count = len(refs) // 2
    for ref, out_ref in zip(refs[:count], refs[count:]):
        value = ref[...]
        norm = split3(jnp.sum(value * value, axis=0, keepdims=True))
        one = jnp.ones((1, value.shape[1]), F32)
        misc = stack_rows((*norm, one, one, one), value.shape[1])
        out_ref[...] = jnp.concatenate([*split3(value), misc], axis=0).astype(BF16)


def row_features(blocks):
    vmem = pl.BlockSpec(memory_space=pltpu.VMEM)
    return pl.pallas_call(
        row_kernel,
        out_shape=tuple(jax.ShapeDtypeStruct((64, block.shape[1]), BF16) for block in blocks),
        in_specs=[vmem] * len(blocks),
        out_specs=(vmem,) * len(blocks),
        compiler_params=pltpu.CompilerParams(vmem_limit_bytes=8 * 2**20),
        name="row_features",
    )(*blocks)


def col_kernel(place_ref, packets_ref, col_f, low):
    yl = place_ref[0]
    pieces = packets_ref.shape[0] // 2
    piece = packets_ref.shape[2] // 3

    def features(p):
        parts = [packets_ref[q * pieces + p].astype(F32) for q in range(2)]
        value = jnp.concatenate([part[:, 2 * piece :] for part in parts], axis=0)
        norm = split3(jnp.sum(value * value, axis=0, keepdims=True))
        one = jnp.ones((1, piece), F32)
        misc = stack_rows((one, one, one, *norm), piece)
        cross = -2.0 * value
        place = pl.ds(pl.multiple_of(p * piece, piece), piece)
        col_f[place, :] = jnp.concatenate([cross, cross, cross, misc], axis=0).T.astype(BF16)
        parts = [packets_ref[q * pieces + p].astype(F32) for q in (yl, 1 - yl)]
        columns = [part[:, k * piece : (k + 1) * piece] for k in range(2) for part in parts]
        low[:, place] = jnp.concatenate(columns, axis=0).astype(BF16)

    def some(index, _):
        for k in range(4):
            features(4 * index + k)
        return 0

    lax.fori_loop(0, pieces // 4, some, 0)


def col_features(place, packets):
    vmem = pl.BlockSpec(memory_space=pltpu.VMEM)
    count = packets.shape[0] * packets.shape[2] // 6
    return pl.pallas_call(
        col_kernel,
        out_shape=(jax.ShapeDtypeStruct((count, 64), BF16), jax.ShapeDtypeStruct((32, count), BF16)),
        in_specs=[pl.BlockSpec(memory_space=pltpu.SMEM), vmem],
        out_specs=(vmem, vmem),
        compiler_params=pltpu.CompilerParams(vmem_limit_bytes=8 * 2**20),
        name="col_features",
    )(place, packets)


def image_kernel(groups, sets, tile_i, tile_j, more, *refs):
    rows_refs, refs = refs[:groups], refs[groups:]
    col_refs, low_refs, refs = refs[:sets], refs[sets : 2 * sets], refs[2 * sets :]
    start_refs, refs = refs[: groups * more], refs[groups * more :]
    out_refs, (rows, col_f, low, total, dist_s, expo_s, kern_s) = refs[:groups], refs[groups:]
    part_j, count_j = low_refs[0].shape[1], low.shape[1]
    width = out_refs[0].shape[1]
    count_i = groups * width
    for g in range(groups):
        rows[:, g * width : (g + 1) * width] = rows_refs[g][...]
    for k in range(sets):
        col_f[k * part_j : (k + 1) * part_j, :] = col_refs[k][...]
        low[:, k * part_j : (k + 1) * part_j] = low_refs[k][...]
    per = count_j // tile_j
    steps = (count_i // tile_i) * per
    per_group = width // tile_i

    def spot_i(step):
        return pl.ds(pl.multiple_of((step // per) * tile_i, tile_i), tile_i)

    def spot_j(step):
        return pl.ds(pl.multiple_of((step % per) * tile_j, tile_j), tile_j)

    def distances(step, slot):
        dist_s[slot] = jnp.dot(
            col_f[spot_j(step), :], rows[:, spot_i(step)], preferred_element_type=F32
        )

    def exponents(slot, a):
        dist = jnp.maximum(dist_s[slot, a : a + 16, :], TINY)
        expo_s[slot, a : a + 16, :] = SHIFT - dist * lax.rsqrt(dist)

    def entries(slot, a):
        t = expo_s[slot, a : a + 16, :]
        kern_s[slot, a : a + 16, :] = ((t * t + CONST) * jnp.exp2(t)).astype(BF16)

    def accumulate(step, slot):
        tile = step // per
        group = tile // per_group
        place = pl.ds(pl.multiple_of((tile % per_group) * tile_i, tile_i), tile_i)
        product = jnp.dot(low[:, spot_j(step)], kern_s[slot], preferred_element_type=F32)
        total[group, :, place] += product

    for g in range(groups):
        total[g] = start_refs[g][...] if more else jnp.zeros_like(total[g])
    kern_s[1] = jnp.zeros((tile_j, tile_i), BF16)
    distances(0, 0)
    distances(1, 1)
    for a in range(0, tile_j, 16):
        exponents(0, a)

    def one(step, slot):
        accumulate(jnp.maximum(step - 1, 0), 1 - slot)
        for a in range(0, tile_j, 16):
            entries(slot, a)
            exponents(1 - slot, a)
        distances(jnp.minimum(step + 2, steps - 1), slot)

    def four(index, _):
        for k in range(4):
            one(4 * index + k, k % 2)
        return 0

    lax.fori_loop(0, steps // 4, four, 0)
    accumulate(steps - 1, 1)
    for g in range(groups):
        out_refs[g][...] = total[g]


def kernel_image(rows, columns, start=(), tile_i=256, tile_j=1024):
    cols, lows = zip(*columns)
    groups, sets, width = len(rows), len(cols), rows[0].shape[1]
    count_i, count_j = groups * width, sets * lows[0].shape[1]
    vmem = pl.BlockSpec(memory_space=pltpu.VMEM)
    return pl.pallas_call(
        functools.partial(image_kernel, groups, sets, tile_i, tile_j, len(start) > 0),
        out_shape=(jax.ShapeDtypeStruct((32, width), F32),) * groups,
        in_specs=[vmem] * (groups + 2 * sets + len(start)),
        out_specs=(vmem,) * groups,
        scratch_shapes=[
            pltpu.VMEM((64, count_i), BF16),
            pltpu.VMEM((count_j, 64), BF16),
            pltpu.VMEM((32, count_j), BF16),
            pltpu.VMEM((groups, 32, width), F32),
            pltpu.VMEM((2, tile_j, tile_i), F32),
            pltpu.VMEM((2, tile_j, tile_i), F32),
            pltpu.VMEM((2, tile_j, tile_i), BF16),
        ],
        compiler_params=pltpu.CompilerParams(vmem_limit_bytes=24 * 2**20),
        cost_estimate=pl.CostEstimate(
            flops=2 * count_i * count_j * 96,
            bytes_accessed=4 * 1024 * 1024,
            transcendentals=2 * count_i * count_j,
        ),
        name="kernel_image",
    )(*rows, *cols, *lows, *start)


def add_kernel(count, *refs):
    total = refs[0][...]
    for ref in refs[1:count]:
        total = total + ref[...]
    half = total.shape[0] // 2
    refs[count][...] = total[:half]
    refs[count + 1][...] = total[half:]


def add_parts(parts):
    vmem = pl.BlockSpec(memory_space=pltpu.VMEM)
    columns, width = parts[0].shape
    return pl.pallas_call(
        functools.partial(add_kernel, len(parts)),
        out_shape=(jax.ShapeDtypeStruct((columns // 2, width), F32),) * 2,
        in_specs=[vmem] * len(parts),
        out_specs=(vmem,) * 2,
        compiler_params=pltpu.CompilerParams(vmem_limit_bytes=8 * 2**20),
        name="add_parts",
    )(*parts)


def prepare_kernel(lengths_ref, points_ref, direction_ref, scaled_ref, low_ref):
    dims = points_ref.shape[0]
    index = lax.broadcasted_iota(jnp.int32, (dims, 128), 0)
    lengths = jnp.ones((dims, 128), F32)
    for d in range(dims):
        lengths = jnp.where(index == d, lengths_ref[d], lengths)
    scale = ((KAPPA * math.sqrt(5.0)) / lengths)[:, :1]
    scaled_ref[...] = points_ref[...] * scale
    low_ref[...] = direction_ref[...].astype(BF16)


def prepare(lengths, points, direction):
    vmem = pl.BlockSpec(memory_space=pltpu.VMEM)
    return pl.pallas_call(
        prepare_kernel,
        out_shape=(
            jax.ShapeDtypeStruct(points.shape, F32),
            jax.ShapeDtypeStruct(direction.shape, BF16),
        ),
        in_specs=[pl.BlockSpec(memory_space=pltpu.SMEM), vmem, vmem],
        out_specs=(vmem, vmem),
        compiler_params=pltpu.CompilerParams(vmem_limit_bytes=8 * 2**20),
        name="prepare",
    )(lengths, points, direction)


def pack_kernel(far, place_ref, scaled_ref, low_ref, other_ref, packets_ref):
    yl, core = place_ref[0], place_ref[1]
    piece = low_ref.shape[1] // 4
    for q in range(2):
        here = pl.ds(pl.multiple_of((2 * q + core) * piece, piece), piece)
        half = scaled_ref[pl.ds(pl.multiple_of(yl * 8, 8), 8), here]
        parts = [low_ref[:, here], other_ref[:, here].astype(BF16), half.astype(BF16)]
        packet = jnp.concatenate(parts, axis=1)
        for n in range(far):
            packets_ref[q * far + n] = packet


def pack(far, place, scaled, low, other):
    vmem = pl.BlockSpec(memory_space=pltpu.VMEM)
    own, count = low.shape
    return pl.pallas_call(
        functools.partial(pack_kernel, far),
        out_shape=jax.ShapeDtypeStruct((2 * far, own, 3 * count // 4), BF16),
        in_specs=[pl.BlockSpec(memory_space=pltpu.SMEM), vmem, vmem, vmem],
        out_specs=vmem,
        compiler_params=pltpu.CompilerParams(vmem_limit_bytes=8 * 2**20),
        name="pack",
    )(place, scaled, low, other)


def sums_kernel(scale_ref, noise_ref, direction_ref, residual_ref, solution_ref, *refs):
    parts, (image_ref, same_ref, out_ref) = refs[:-3], refs[-3:]
    direction, residual = direction_ref[...], residual_ref[...]
    total = parts[0][...]
    for part in parts[1:]:
        total = total + part[...]
    image = (FACTOR * scale_ref[0]) * total + noise_ref[...] * direction
    image_ref[...] = image
    same_ref[...] = solution_ref[...]
    own = direction.shape[0]
    lane = lax.broadcasted_iota(jnp.int32, (own, 128), 1)
    row = lax.broadcasted_iota(jnp.int32, (own, 128), 0)
    sums = jnp.zeros((own, 128), F32)
    for k, term in enumerate((residual * residual, direction * image, residual * image, image * image)):
        sums = jnp.where(lane == k * own + row, jnp.sum(term, axis=1, keepdims=True), sums)
    out_ref[...] = jnp.broadcast_to(jnp.sum(sums, axis=0, keepdims=True), out_ref.shape)


def column_sums(scale, parts, noise, direction, residual, solution, copies):
    vmem = pl.BlockSpec(memory_space=pltpu.VMEM)
    block = jax.ShapeDtypeStruct(direction.shape, F32)
    return pl.pallas_call(
        sums_kernel,
        out_shape=(block, block, jax.ShapeDtypeStruct((copies, 128), F32)),
        in_specs=[pl.BlockSpec(memory_space=pltpu.SMEM)] + [vmem] * (4 + len(parts)),
        out_specs=(vmem,) * 3,
        compiler_params=pltpu.CompilerParams(vmem_limit_bytes=8 * 2**20),
        name="column_sums",
    )(scale, noise, direction, residual, solution, *parts)


def local(points, lengths, noise, outscale, solution, residual, direction):
    far, line = lax.axis_size(FAR), lax.axis_size("x")
    own, count = direction.shape
    swap = [(0, 1), (1, 0)]

    place = jnp.stack([lax.axis_index("yl"), lax.axis_index("core")])
    other = lax.ppermute(direction, "core", swap)
    scaled, low = prepare(lengths, points, direction)
    packets = pack(far, place, scaled, low, other)
    packets = lax.all_to_all(packets, ("yl", *FAR), 0, 0, tiled=True)
    blocks = [scaled] + [
        lax.ppermute(scaled, "x", [(i, (i - step) % line) for i in range(line)])
        for step in range(1, line)
    ]
    rows = row_features(blocks)

    def send(value, step):
        return lax.ppermute(value, "x", [(i, (i + step) % line) for i in range(line)])

    packets, *rows = lax.optimization_barrier((packets, *rows))
    near = col_features(place, packets)
    others = kernel_image((rows[3], rows[2], rows[1]), (near,))
    distant = col_features(place, lax.ppermute(packets, "yh", swap))
    image3, image2, image1 = kernel_image((rows[3], rows[2], rows[1]), (distant,), others)
    image3, image2, image1 = send(image3, 3), send(image2, 2), send(image1, 1)
    (image0,) = kernel_image((rows[0],), (near, distant))
    keep, rest = add_parts((image0, image1, image2, image3))
    keep, rest = add_parts((keep, lax.ppermute(rest, "core", swap)))
    parts = [keep, lax.ppermute(rest, "yl", swap)]
    image, solution, sums = column_sums(
        outscale, parts, noise[None, :], direction, residual, solution, lax.axis_size(BLK)
    )
    sums = lax.all_to_all(sums, BLK, 0, 0, tiled=True)
    sums = jnp.sum(sums, axis=0)[: 4 * own].reshape(4, own)
    norm_now, curve, mixed, square = sums[0], sums[1], sums[2], sums[3]
    alpha = norm_now / curve
    norm_next = jnp.maximum(norm_now - alpha * (2.0 * mixed - alpha * square), 0.0)
    solution_next = solution + alpha[:, None] * direction
    residual_next = residual - alpha[:, None] * image
    direction_next = residual_next + (norm_next / norm_now)[:, None] * direction
    return (solution_next, residual_next, direction_next)


def solution(mesh):
    fine = Mesh(mesh.devices.reshape(8, 2, 4, 2, 2), (*BLK, *COL))
    in_specs = (
        P(None, BLK),
        P(),
        P(BLK),
        P(),
        P(COL, BLK),
        P(COL, BLK),
        P(COL, BLK),
    )
    out_specs = (P(COL, BLK), P(COL, BLK), P(COL, BLK))
    return jax.shard_map(local, mesh=fine, in_specs=in_specs, out_specs=out_specs, check_vma=False)
```

```python
import functools
import math

import jax
import jax.numpy as jnp
from jax import lax
from jax.experimental import pallas as pl
from jax.experimental.pallas import tpu as pltpu
from jax.sharding import Mesh, PartitionSpec as P

F32 = jnp.float32
BF16 = jnp.bfloat16
KAPPA = 1.0 / math.log(2.0)
SHIFT = -1.5 * KAPPA
CONST = 0.75 * KAPPA * KAPPA
FACTOR = math.exp(1.5) / (3.0 * KAPPA * KAPPA)
TINY = 1e-30

BLK = ("z", "yh", "x")
COL = ("yl", "core")
FAR = ("z",)


def split3(value):
    high = value.astype(BF16).astype(F32)
    rest = value - high
    middle = rest.astype(BF16).astype(F32)
    return high, middle, rest - middle


def stack_rows(rows, width):
    index = lax.broadcasted_iota(jnp.int32, (16, width), 0)
    total = jnp.zeros((16, width), F32)
    for place, row in enumerate(rows):
        total = jnp.where(index == place, row, total)
    return total


def row_kernel(*refs):
    count = len(refs) // 2
    for ref, out_ref in zip(refs[:count], refs[count:]):
        value = ref[...]
        norm = split3(jnp.sum(value * value, axis=0, keepdims=True))
        one = jnp.ones((1, value.shape[1]), F32)
        misc = stack_rows((*norm, one, one, one), value.shape[1])
        out_ref[...] = jnp.concatenate([*split3(value), misc], axis=0).astype(BF16)


def row_features(blocks):
    vmem = pl.BlockSpec(memory_space=pltpu.VMEM)
    return pl.pallas_call(
        row_kernel,
        out_shape=tuple(jax.ShapeDtypeStruct((64, block.shape[1]), BF16) for block in blocks),
        in_specs=[vmem] * len(blocks),
        out_specs=(vmem,) * len(blocks),
        compiler_params=pltpu.CompilerParams(vmem_limit_bytes=8 * 2**20),
        name="row_features",
    )(*blocks)


def col_kernel(place_ref, packets_ref, col_f, low):
    yl = place_ref[0]
    pieces = packets_ref.shape[0] // 2
    piece = packets_ref.shape[2] // 3

    def features(p):
        parts = [packets_ref[q * pieces + p].astype(F32) for q in range(2)]
        value = jnp.concatenate([part[:, 2 * piece :] for part in parts], axis=0)
        norm = split3(jnp.sum(value * value, axis=0, keepdims=True))
        one = jnp.ones((1, piece), F32)
        misc = stack_rows((one, one, one, *norm), piece)
        cross = -2.0 * value
        place = slice(p * piece, (p + 1) * piece)
        col_f[place, :] = jnp.concatenate([cross, cross, cross, misc], axis=0).T.astype(BF16)
        parts = [packets_ref[q * pieces + p].astype(F32) for q in (yl, 1 - yl)]
        columns = [part[:, k * piece : (k + 1) * piece] for k in range(2) for part in parts]
        low[:, place] = jnp.concatenate(columns, axis=0).astype(BF16)

    for p in range(pieces):
        features(p)


def col_features(place, packets):
    vmem = pl.BlockSpec(memory_space=pltpu.VMEM)
    count = packets.shape[0] * packets.shape[2] // 6
    return pl.pallas_call(
        col_kernel,
        out_shape=(jax.ShapeDtypeStruct((count, 64), BF16), jax.ShapeDtypeStruct((32, count), BF16)),
        in_specs=[pl.BlockSpec(memory_space=pltpu.SMEM), vmem],
        out_specs=(vmem, vmem),
        compiler_params=pltpu.CompilerParams(vmem_limit_bytes=8 * 2**20),
        name="col_features",
    )(place, packets)


def image_kernel(groups, sets, tile_i, tile_j, more, *refs):
    rows_refs, refs = refs[:groups], refs[groups:]
    col_refs, low_refs, refs = refs[:sets], refs[sets : 2 * sets], refs[2 * sets :]
    start_refs, refs = refs[: groups * more], refs[groups * more :]
    out_refs, (rows, col_f, low, total, dist_s, expo_s, kern_s) = refs[:groups], refs[groups:]
    part_j, count_j = low_refs[0].shape[1], low.shape[1]
    width = out_refs[0].shape[1]
    count_i = groups * width
    if groups == 1:
        rows = rows_refs[0]
    else:
        for g in range(groups):
            rows[:, g * width : (g + 1) * width] = rows_refs[g][...]
    if sets == 1:
        col_f, low = col_refs[0], low_refs[0]
    else:
        for k in range(sets):
            col_f[k * part_j : (k + 1) * part_j, :] = col_refs[k][...]
            low[:, k * part_j : (k + 1) * part_j] = low_refs[k][...]
    per = count_j // tile_j
    steps = (count_i // tile_i) * per
    per_group = width // tile_i

    def spot_i(step):
        return pl.ds(pl.multiple_of((step // per) * tile_i, tile_i), tile_i)

    def spot_j(step):
        return pl.ds(pl.multiple_of((step % per) * tile_j, tile_j), tile_j)

    def distances(step, slot):
        dist_s[slot] = jnp.dot(
            col_f[spot_j(step), :], rows[:, spot_i(step)], preferred_element_type=F32
        )

    def exponents(slot, a):
        dist = jnp.maximum(dist_s[slot, a : a + 16, :], TINY)
        expo_s[slot, a : a + 16, :] = SHIFT - dist * lax.rsqrt(dist)

    def entries(slot, a):
        t = expo_s[slot, a : a + 16, :]
        kern_s[slot, a : a + 16, :] = ((t * t + CONST) * jnp.exp2(t)).astype(BF16)

    def accumulate(step, slot):
        tile = step // per
        group = tile // per_group
        place = pl.ds(pl.multiple_of((tile % per_group) * tile_i, tile_i), tile_i)
        product = jnp.dot(low[:, spot_j(step)], kern_s[slot], preferred_element_type=F32)
        total[group, :, place] += product

    for g in range(groups):
        total[g] = start_refs[g][...] if more else jnp.zeros_like(total[g])
    kern_s[1] = jnp.zeros((tile_j, tile_i), BF16)
    distances(0, 0)
    distances(1, 1)
    for a in range(0, tile_j, 16):
        exponents(0, a)

    def one(step, slot):
        accumulate(jnp.maximum(step - 1, 0), 1 - slot)
        for a in range(0, tile_j, 16):
            entries(slot, a)
            exponents(1 - slot, a)
        distances(jnp.minimum(step + 2, steps - 1), slot)

    def four(index, _):
        for k in range(4):
            one(4 * index + k, k % 2)
        return 0

    lax.fori_loop(0, steps // 4, four, 0)
    accumulate(steps - 1, 1)
    for g in range(groups):
        out_refs[g][...] = total[g]


def kernel_image(rows, columns, start=(), tile_i=256, tile_j=1024):
    cols, lows = zip(*columns)
    groups, sets, width = len(rows), len(cols), rows[0].shape[1]
    count_i, count_j = groups * width, sets * lows[0].shape[1]
    vmem = pl.BlockSpec(memory_space=pltpu.VMEM)
    return pl.pallas_call(
        functools.partial(image_kernel, groups, sets, tile_i, tile_j, len(start) > 0),
        out_shape=(jax.ShapeDtypeStruct((32, width), F32),) * groups,
        in_specs=[vmem] * (groups + 2 * sets + len(start)),
        out_specs=(vmem,) * groups,
        scratch_shapes=[
            pltpu.VMEM((64, count_i), BF16),
            pltpu.VMEM((count_j, 64), BF16),
            pltpu.VMEM((32, count_j), BF16),
            pltpu.VMEM((groups, 32, width), F32),
            pltpu.VMEM((2, tile_j, tile_i), F32),
            pltpu.VMEM((2, tile_j, tile_i), F32),
            pltpu.VMEM((2, tile_j, tile_i), BF16),
        ],
        compiler_params=pltpu.CompilerParams(vmem_limit_bytes=24 * 2**20),
        cost_estimate=pl.CostEstimate(
            flops=2 * count_i * count_j * 96,
            bytes_accessed=4 * 1024 * 1024,
            transcendentals=2 * count_i * count_j,
        ),
        name="kernel_image",
    )(*rows, *cols, *lows, *start)


def add_kernel(count, *refs):
    total = refs[0][...]
    for ref in refs[1:count]:
        total = total + ref[...]
    half = total.shape[0] // 2
    refs[count][...] = total[:half]
    refs[count + 1][...] = total[half:]


def add_parts(parts):
    vmem = pl.BlockSpec(memory_space=pltpu.VMEM)
    columns, width = parts[0].shape
    return pl.pallas_call(
        functools.partial(add_kernel, len(parts)),
        out_shape=(jax.ShapeDtypeStruct((columns // 2, width), F32),) * 2,
        in_specs=[vmem] * len(parts),
        out_specs=(vmem,) * 2,
        compiler_params=pltpu.CompilerParams(vmem_limit_bytes=8 * 2**20),
        name="add_parts",
    )(*parts)


def prepare_kernel(lengths_ref, points_ref, direction_ref, scaled_ref, low_ref):
    dims = points_ref.shape[0]
    index = lax.broadcasted_iota(jnp.int32, (dims, 128), 0)
    lengths = jnp.ones((dims, 128), F32)
    for d in range(dims):
        lengths = jnp.where(index == d, lengths_ref[d], lengths)
    scale = ((KAPPA * math.sqrt(5.0)) / lengths)[:, :1]
    scaled_ref[...] = points_ref[...] * scale
    low_ref[...] = direction_ref[...].astype(BF16)


def prepare(lengths, points, direction):
    vmem = pl.BlockSpec(memory_space=pltpu.VMEM)
    return pl.pallas_call(
        prepare_kernel,
        out_shape=(
            jax.ShapeDtypeStruct(points.shape, F32),
            jax.ShapeDtypeStruct(direction.shape, BF16),
        ),
        in_specs=[pl.BlockSpec(memory_space=pltpu.SMEM), vmem, vmem],
        out_specs=(vmem, vmem),
        compiler_params=pltpu.CompilerParams(vmem_limit_bytes=8 * 2**20),
        name="prepare",
    )(lengths, points, direction)


def pack_kernel(far, place_ref, scaled_ref, low_ref, other_ref, packets_ref):
    yl, core = place_ref[0], place_ref[1]
    piece = low_ref.shape[1] // 4
    for q in range(2):
        here = pl.ds(pl.multiple_of((2 * q + core) * piece, piece), piece)
        half = scaled_ref[pl.ds(pl.multiple_of(yl * 8, 8), 8), here]
        parts = [low_ref[:, here], other_ref[:, here].astype(BF16), half.astype(BF16)]
        packet = jnp.concatenate(parts, axis=1)
        for n in range(far):
            packets_ref[q * far + n] = packet


def pack(far, place, scaled, low, other):
    vmem = pl.BlockSpec(memory_space=pltpu.VMEM)
    own, count = low.shape
    return pl.pallas_call(
        functools.partial(pack_kernel, far),
        out_shape=jax.ShapeDtypeStruct((2 * far, own, 3 * count // 4), BF16),
        in_specs=[pl.BlockSpec(memory_space=pltpu.SMEM), vmem, vmem, vmem],
        out_specs=vmem,
        compiler_params=pltpu.CompilerParams(vmem_limit_bytes=8 * 2**20),
        name="pack",
    )(place, scaled, low, other)


def sums_kernel(scale_ref, noise_ref, direction_ref, residual_ref, solution_ref, *refs):
    parts, (image_ref, same_ref, out_ref) = refs[:-3], refs[-3:]
    direction, residual = direction_ref[...], residual_ref[...]
    total = parts[0][...]
    for part in parts[1:]:
        total = total + part[...]
    image = (FACTOR * scale_ref[0]) * total + noise_ref[...] * direction
    image_ref[...] = image
    same_ref[...] = solution_ref[...]
    own = direction.shape[0]
    lane = lax.broadcasted_iota(jnp.int32, (own, 128), 1)
    row = lax.broadcasted_iota(jnp.int32, (own, 128), 0)
    sums = jnp.zeros((own, 128), F32)
    for k, term in enumerate((residual * residual, direction * image, residual * image, image * image)):
        sums = jnp.where(lane == k * own + row, jnp.sum(term, axis=1, keepdims=True), sums)
    out_ref[...] = jnp.broadcast_to(jnp.sum(sums, axis=0, keepdims=True), out_ref.shape)


def column_sums(scale, parts, noise, direction, residual, solution, copies):
    vmem = pl.BlockSpec(memory_space=pltpu.VMEM)
    block = jax.ShapeDtypeStruct(direction.shape, F32)
    return pl.pallas_call(
        sums_kernel,
        out_shape=(block, block, jax.ShapeDtypeStruct((copies, 128), F32)),
        in_specs=[pl.BlockSpec(memory_space=pltpu.SMEM)] + [vmem] * (4 + len(parts)),
        out_specs=(vmem,) * 3,
        compiler_params=pltpu.CompilerParams(vmem_limit_bytes=8 * 2**20),
        name="column_sums",
    )(scale, noise, direction, residual, solution, *parts)


def local(points, lengths, noise, outscale, solution, residual, direction):
    far, line = lax.axis_size(FAR), lax.axis_size("x")
    own, count = direction.shape
    swap = [(0, 1), (1, 0)]

    place = jnp.stack([lax.axis_index("yl"), lax.axis_index("core")])
    other = lax.ppermute(direction, "core", swap)
    scaled, low = prepare(lengths, points, direction)
    packets = pack(far, place, scaled, low, other)
    packets = lax.all_to_all(packets, ("yl", *FAR), 0, 0, tiled=True)
    blocks = [scaled] + [
        lax.ppermute(scaled, "x", [(i, i ^ step) for i in range(line)])
        for step in range(1, line)
    ]
    rows = row_features(blocks)

    def send(value, step):
        return lax.ppermute(value, "x", [(i, i ^ step) for i in range(line)])

    packets, *rows = lax.optimization_barrier((packets, *rows))
    near = col_features(place, packets)
    others = kernel_image((rows[3], rows[2], rows[1]), (near,))
    distant = col_features(place, lax.ppermute(packets, "yh", swap))
    image3, image2, image1 = kernel_image((rows[3], rows[2], rows[1]), (distant,), others)
    image3, image2, image1 = send(image3, 3), send(image2, 2), send(image1, 1)
    (image0,) = kernel_image((rows[0],), (near, distant))
    keep, rest = add_parts((image0, image1, image2, image3))
    keep, rest = add_parts((keep, lax.ppermute(rest, "core", swap)))
    parts = [keep, lax.ppermute(rest, "yl", swap)]
    image, solution, sums = column_sums(
        outscale, parts, noise[None, :], direction, residual, solution, lax.axis_size(BLK)
    )
    sums = lax.all_to_all(sums, BLK, 0, 0, tiled=True)
    sums = jnp.sum(sums, axis=0)[: 4 * own].reshape(4, own)
    norm_now, curve, mixed, square = sums[0], sums[1], sums[2], sums[3]
    alpha = norm_now / curve
    norm_next = jnp.maximum(norm_now - alpha * (2.0 * mixed - alpha * square), 0.0)
    solution_next = solution + alpha[:, None] * direction
    residual_next = residual - alpha[:, None] * image
    direction_next = residual_next + (norm_next / norm_now)[:, None] * direction
    return (solution_next, residual_next, direction_next)


def solution(mesh):
    fine = Mesh(mesh.devices.reshape(8, 2, 4, 2, 2), (*BLK, *COL))
    in_specs = (
        P(None, BLK),
        P(),
        P(BLK),
        P(),
        P(COL, BLK),
        P(COL, BLK),
        P(COL, BLK),
    )
    out_specs = (P(COL, BLK), P(COL, BLK), P(COL, BLK))
    return jax.shard_map(local, mesh=fine, in_specs=in_specs, out_specs=out_specs, check_vma=False)
```

```python
import functools
import math

import jax
import jax.numpy as jnp
from jax import lax
from jax.experimental import pallas as pl
from jax.experimental.pallas import tpu as pltpu
from jax.sharding import Mesh, PartitionSpec as P

F32 = jnp.float32
BF16 = jnp.bfloat16
KAPPA = 1.0 / math.log(2.0)
SHIFT = -1.5 * KAPPA
CONST = 0.75 * KAPPA * KAPPA
FACTOR = math.exp(1.5) / (3.0 * KAPPA * KAPPA)
TINY = 1e-30

BLK = ("z", "yh", "x")
COL = ("yl", "core")
FAR = ("z",)


def split3(value):
    high = value.astype(BF16).astype(F32)
    rest = value - high
    middle = rest.astype(BF16).astype(F32)
    return high, middle, rest - middle


def stack_rows(rows, width):
    index = lax.broadcasted_iota(jnp.int32, (16, width), 0)
    total = jnp.zeros((16, width), F32)
    for place, row in enumerate(rows):
        total = jnp.where(index == place, row, total)
    return total


def row_kernel(scale_ref, *refs):
    count = len(refs) // 2
    scale = scale_ref[:, :1]
    for ref, out_ref in zip(refs[:count], refs[count:]):
        value = ref[...] * scale
        norm = split3(jnp.sum(value * value, axis=0, keepdims=True))
        one = jnp.ones((1, value.shape[1]), F32)
        misc = stack_rows((*norm, one, one, one), value.shape[1])
        out_ref[...] = jnp.concatenate([*split3(value * scale), misc], axis=0).astype(BF16)


def row_features(scale, blocks):
    vmem = pl.BlockSpec(memory_space=pltpu.VMEM)
    return pl.pallas_call(
        row_kernel,
        out_shape=tuple(jax.ShapeDtypeStruct((64, block.shape[1]), BF16) for block in blocks),
        in_specs=[vmem] * (len(blocks) + 1),
        out_specs=(vmem,) * len(blocks),
        compiler_params=pltpu.CompilerParams(vmem_limit_bytes=8 * 2**20),
        name="row_features",
    )(scale, *blocks)


def col_kernel(place_ref, scale_ref, packets_ref, col_f, low):
    yl = place_ref[0]
    pieces = packets_ref.shape[0] // 2
    piece = packets_ref.shape[2] // 3

    def features(p):
        parts = [packets_ref[q * pieces + p].astype(F32) for q in range(2)]
        value = jnp.concatenate([part[:, 2 * piece :] for part in parts], axis=0)
        scaled = value * scale_ref[:, :1]
        norm = split3(jnp.sum(scaled * scaled, axis=0, keepdims=True))
        one = jnp.ones((1, piece), F32)
        misc = stack_rows((one, one, one, *norm), piece)
        cross = -2.0 * value
        place = slice(p * piece, (p + 1) * piece)
        col_f[place, :] = jnp.concatenate([cross, cross, cross, misc], axis=0).T.astype(BF16)
        parts = [packets_ref[q * pieces + p].astype(F32) for q in (yl, 1 - yl)]
        columns = [part[:, k * piece : (k + 1) * piece] for k in range(2) for part in parts]
        low[:, place] = jnp.concatenate(columns, axis=0).astype(BF16)

    for p in range(pieces):
        features(p)


def col_features(place, scale, packets):
    vmem = pl.BlockSpec(memory_space=pltpu.VMEM)
    count = packets.shape[0] * packets.shape[2] // 6
    return pl.pallas_call(
        col_kernel,
        out_shape=(jax.ShapeDtypeStruct((count, 64), BF16), jax.ShapeDtypeStruct((32, count), BF16)),
        in_specs=[pl.BlockSpec(memory_space=pltpu.SMEM), vmem, vmem],
        out_specs=(vmem, vmem),
        compiler_params=pltpu.CompilerParams(vmem_limit_bytes=8 * 2**20),
        name="col_features",
    )(place, scale, packets)


def image_kernel(groups, sets, tile_i, tile_j, more, *refs):
    rows_refs, refs = refs[:groups], refs[groups:]
    col_refs, low_refs, refs = refs[:sets], refs[sets : 2 * sets], refs[2 * sets :]
    start_refs, refs = refs[: groups * more], refs[groups * more :]
    out_refs, (rows, col_f, low, total, dist_s, expo_s, kern_s) = refs[:groups], refs[groups:]
    part_j, count_j = low_refs[0].shape[1], low.shape[1]
    width = out_refs[0].shape[1]
    count_i = groups * width
    if groups == 1:
        rows = rows_refs[0]
    else:
        for g in range(groups):
            rows[:, g * width : (g + 1) * width] = rows_refs[g][...]
    if sets == 1:
        col_f, low = col_refs[0], low_refs[0]
    else:
        for k in range(sets):
            col_f[k * part_j : (k + 1) * part_j, :] = col_refs[k][...]
            low[:, k * part_j : (k + 1) * part_j] = low_refs[k][...]
    per = count_j // tile_j
    steps = (count_i // tile_i) * per
    per_group = width // tile_i

    def spot_i(step):
        return pl.ds(pl.multiple_of((step // per) * tile_i, tile_i), tile_i)

    def spot_j(step):
        return pl.ds(pl.multiple_of((step % per) * tile_j, tile_j), tile_j)

    def distances(step, slot):
        dist_s[slot] = jnp.dot(
            col_f[spot_j(step), :], rows[:, spot_i(step)], preferred_element_type=F32
        )

    def exponents(slot, a):
        dist = jnp.maximum(dist_s[slot, a : a + 16, :], TINY)
        expo_s[slot, a : a + 16, :] = SHIFT - dist * lax.rsqrt(dist)

    def entries(slot, a):
        t = expo_s[slot, a : a + 16, :]
        kern_s[slot, a : a + 16, :] = ((t * t + CONST) * jnp.exp2(t)).astype(BF16)

    def accumulate(step, slot):
        tile = step // per
        group = tile // per_group
        place = pl.ds(pl.multiple_of((tile % per_group) * tile_i, tile_i), tile_i)
        product = jnp.dot(low[:, spot_j(step)], kern_s[slot], preferred_element_type=F32)
        total[group, :, place] += product

    for g in range(groups):
        total[g] = start_refs[g][...] if more else jnp.zeros_like(total[g])
    kern_s[1] = jnp.zeros((tile_j, tile_i), BF16)
    distances(0, 0)
    distances(1, 1)
    for a in range(0, tile_j, 16):
        exponents(0, a)

    def one(step, slot):
        accumulate(jnp.maximum(step - 1, 0), 1 - slot)
        for a in range(0, tile_j, 16):
            entries(slot, a)
            exponents(1 - slot, a)
        distances(jnp.minimum(step + 2, steps - 1), slot)

    def four(index, _):
        for k in range(4):
            one(4 * index + k, k % 2)
        return 0

    lax.fori_loop(0, steps // 4, four, 0)
    accumulate(steps - 1, 1)
    for g in range(groups):
        out_refs[g][...] = total[g]


def kernel_image(rows, columns, start=(), tile_i=256, tile_j=1024):
    cols, lows = zip(*columns)
    groups, sets, width = len(rows), len(cols), rows[0].shape[1]
    count_i, count_j = groups * width, sets * lows[0].shape[1]
    vmem = pl.BlockSpec(memory_space=pltpu.VMEM)
    return pl.pallas_call(
        functools.partial(image_kernel, groups, sets, tile_i, tile_j, len(start) > 0),
        out_shape=(jax.ShapeDtypeStruct((32, width), F32),) * groups,
        in_specs=[vmem] * (groups + 2 * sets + len(start)),
        out_specs=(vmem,) * groups,
        scratch_shapes=[
            pltpu.VMEM((64, count_i), BF16),
            pltpu.VMEM((count_j, 64), BF16),
            pltpu.VMEM((32, count_j), BF16),
            pltpu.VMEM((groups, 32, width), F32),
            pltpu.VMEM((2, tile_j, tile_i), F32),
            pltpu.VMEM((2, tile_j, tile_i), F32),
            pltpu.VMEM((2, tile_j, tile_i), BF16),
        ],
        compiler_params=pltpu.CompilerParams(vmem_limit_bytes=24 * 2**20),
        cost_estimate=pl.CostEstimate(
            flops=2 * count_i * count_j * 96,
            bytes_accessed=4 * 1024 * 1024,
            transcendentals=2 * count_i * count_j,
        ),
        name="kernel_image",
    )(*rows, *cols, *lows, *start)


def add_kernel(count, *refs):
    total = refs[0][...]
    for ref in refs[1:count]:
        total = total + ref[...]
    half = total.shape[0] // 2
    refs[count][...] = total[:half]
    refs[count + 1][...] = total[half:]


def add_parts(parts):
    vmem = pl.BlockSpec(memory_space=pltpu.VMEM)
    columns, width = parts[0].shape
    return pl.pallas_call(
        functools.partial(add_kernel, len(parts)),
        out_shape=(jax.ShapeDtypeStruct((columns // 2, width), F32),) * 2,
        in_specs=[vmem] * len(parts),
        out_specs=(vmem,) * 2,
        compiler_params=pltpu.CompilerParams(vmem_limit_bytes=8 * 2**20),
        name="add_parts",
    )(*parts)


def prepare_kernel(place_ref, points_ref, direction_ref, half_ref, low_ref):
    half_ref[...] = points_ref[pl.ds(pl.multiple_of(place_ref[0] * 8, 8), 8), :]
    low_ref[...] = direction_ref[...].astype(BF16)


def prepare(place, points, direction):
    vmem = pl.BlockSpec(memory_space=pltpu.VMEM)
    return pl.pallas_call(
        prepare_kernel,
        out_shape=(
            jax.ShapeDtypeStruct((8, points.shape[1]), F32),
            jax.ShapeDtypeStruct(direction.shape, BF16),
        ),
        in_specs=[pl.BlockSpec(memory_space=pltpu.SMEM), vmem, vmem],
        out_specs=(vmem, vmem),
        compiler_params=pltpu.CompilerParams(vmem_limit_bytes=8 * 2**20),
        name="prepare",
    )(place, points, direction)


def pack_kernel(far, place_ref, half_ref, low_ref, other_ref, packets_ref):
    core = place_ref[1]
    piece = low_ref.shape[1] // 4
    for q in range(2):
        here = pl.ds(pl.multiple_of((2 * q + core) * piece, piece), piece)
        parts = [low_ref[:, here], other_ref[:, here].astype(BF16), half_ref[:, here].astype(BF16)]
        packet = jnp.concatenate(parts, axis=1)
        for n in range(far):
            packets_ref[q * far + n] = packet


def pack(far, place, half, low, other):
    vmem = pl.BlockSpec(memory_space=pltpu.VMEM)
    own, count = low.shape
    return pl.pallas_call(
        functools.partial(pack_kernel, far),
        out_shape=jax.ShapeDtypeStruct((2 * far, own, 3 * count // 4), BF16),
        in_specs=[pl.BlockSpec(memory_space=pltpu.SMEM), vmem, vmem, vmem],
        out_specs=vmem,
        compiler_params=pltpu.CompilerParams(vmem_limit_bytes=8 * 2**20),
        name="pack",
    )(place, half, low, other)


def sums_kernel(scale_ref, noise_ref, direction_ref, residual_ref, solution_ref, *refs):
    parts, (image_ref, same_ref, out_ref) = refs[:-3], refs[-3:]
    direction, residual = direction_ref[...], residual_ref[...]
    total = parts[0][...]
    for part in parts[1:]:
        total = total + part[...]
    image = (FACTOR * scale_ref[0]) * total + noise_ref[...] * direction
    image_ref[...] = image
    same_ref[...] = solution_ref[...]
    own = direction.shape[0]
    lane = lax.broadcasted_iota(jnp.int32, (own, 128), 1)
    row = lax.broadcasted_iota(jnp.int32, (own, 128), 0)
    sums = jnp.zeros((own, 128), F32)
    for k, term in enumerate((residual * residual, direction * image, residual * image, image * image)):
        sums = jnp.where(lane == k * own + row, jnp.sum(term, axis=1, keepdims=True), sums)
    out_ref[...] = jnp.broadcast_to(jnp.sum(sums, axis=0, keepdims=True), out_ref.shape)


def column_sums(scale, parts, noise, direction, residual, solution, copies):
    vmem = pl.BlockSpec(memory_space=pltpu.VMEM)
    block = jax.ShapeDtypeStruct(direction.shape, F32)
    return pl.pallas_call(
        sums_kernel,
        out_shape=(block, block, jax.ShapeDtypeStruct((copies, 128), F32)),
        in_specs=[pl.BlockSpec(memory_space=pltpu.SMEM)] + [vmem] * (4 + len(parts)),
        out_specs=(vmem,) * 3,
        compiler_params=pltpu.CompilerParams(vmem_limit_bytes=8 * 2**20),
        name="column_sums",
    )(scale, noise, direction, residual, solution, *parts)


def local(points, lengths, noise, outscale, solution, residual, direction):
    far, line = lax.axis_size(FAR), lax.axis_size("x")
    own, count = direction.shape
    swap = [(0, 1), (1, 0)]

    place = jnp.stack([lax.axis_index("yl"), lax.axis_index("core")])
    other = lax.ppermute(direction, "core", swap)
    half, low = prepare(place, points, direction)
    packets = pack(far, place, half, low, other)
    packets = lax.all_to_all(packets, ("yl", *FAR), 0, 0, tiled=True)
    blocks = [points] + [
        lax.ppermute(points, "x", [(i, i ^ step) for i in range(line)])
        for step in range(1, line)
    ]
    factor = (KAPPA * math.sqrt(5.0)) / lengths
    scale = jnp.broadcast_to(factor[:, None], (lengths.shape[0], 128))
    rows = row_features(scale, blocks)

    def send(value, step):
        return lax.ppermute(value, "x", [(i, i ^ step) for i in range(line)])

    packets, scale, *rows = lax.optimization_barrier((packets, scale, *rows))
    near = col_features(place, scale, packets)
    others = kernel_image((rows[3], rows[2], rows[1]), (near,))
    distant = col_features(place, scale, lax.ppermute(packets, "yh", swap))
    image3, image2, image1 = kernel_image((rows[3], rows[2], rows[1]), (distant,), others)
    image3, image2, image1 = send(image3, 3), send(image2, 2), send(image1, 1)
    (image0,) = kernel_image((rows[0],), (near, distant))
    keep, rest = add_parts((image0, image1, image2, image3))
    keep, rest = add_parts((keep, lax.ppermute(rest, "core", swap)))
    parts = [keep, lax.ppermute(rest, "yl", swap)]
    image, solution, sums = column_sums(
        outscale, parts, noise[None, :], direction, residual, solution, lax.axis_size(BLK)
    )
    sums = lax.all_to_all(sums, BLK, 0, 0, tiled=True)
    sums = jnp.sum(sums, axis=0)[: 4 * own].reshape(4, own)
    norm_now, curve, mixed, square = sums[0], sums[1], sums[2], sums[3]
    alpha = norm_now / curve
    norm_next = jnp.maximum(norm_now - alpha * (2.0 * mixed - alpha * square), 0.0)
    solution_next = solution + alpha[:, None] * direction
    residual_next = residual - alpha[:, None] * image
    direction_next = residual_next + (norm_next / norm_now)[:, None] * direction
    return (solution_next, residual_next, direction_next)


def solution(mesh):
    fine = Mesh(mesh.devices.reshape(8, 2, 4, 2, 2), (*BLK, *COL))
    in_specs = (
        P(None, BLK),
        P(),
        P(BLK),
        P(),
        P(COL, BLK),
        P(COL, BLK),
        P(COL, BLK),
    )
    out_specs = (P(COL, BLK), P(COL, BLK), P(COL, BLK))
    return jax.shard_map(local, mesh=fine, in_specs=in_specs, out_specs=out_specs, check_vma=False)
```
